32 devices in a mesh: groups: 2 (over y), date: 4 (over z), tile: 2 (over x), head: 2 (over core).
Axes of the slice: x: 2, y: 2, z: 4, core: 2. Of those that a mesh axis runs over, the one named last changes fastest.
Arguments:
- tokens: bfloat16 [8, 8, 8, 64, 256], P('groups', 'tile', None, 'date'), parts along dimension 0, may hold values from -240 to 240
- cloud_mask: int32 [8, 8, 8, 64], P('groups', 'tile', None, 'date'), parts along dimension 0, may hold values from 0 to 1, as said below
- day_of_year: int32 [128], P(('groups', 'date')), parts along dimension 0, may hold values from 0 to 1460
- query: float32 [256], P('head'), may hold values from -6 to 6
- key_weight: bfloat16 [256, 256], P(None, 'head'), may hold values from -0.375 to 0.375
- value_weight: bfloat16 [256, 256], P(None, 'head'), may hold values from -0.375 to 0.375
- conv_first: bfloat16 [3, 3, 256, 256], P(None, None, None, 'head'), may hold values from -0.375 to 0.375
- conv_second: bfloat16 [3, 3, 256, 256], P(None, None, None, 'head'), may hold values from -0.1875 to 0.1875
Outputs:
- feature_map: bfloat16 [8, 8, 8, 256], P(('groups', 'date'), 'tile', None, 'head'), parts along dimension 0
The draws below stay inside these ranges and needn't reach their ends.
There are 2 independent parts, one for each index of `groups`. The reference program is written for one: setup_inputs(seed, part) draws one part's arguments, and reference() takes and returns one part's arrays. A program takes and returns all parts, laid end to end along the dimension named above; an argument that names none is the same for every part. Nothing has to cross between parts.
Inputs may be any that keep to these rules, and one draw needn't show every extreme that they name: `cloud_mask`: a pixel may be clouded on all 64 dates.
All inputs are finite; a program needn't handle non-finite values.
Results may differ from the reference program's by a relative error of at most 0.012.
The reference program's roundings to bfloat16 on the way (of `inputs`, `pooled` and `hidden`) count: a program that leaves them out, or rounds other values in their place, can miss the bound.
Values may be sent and summed in bfloat16 or wider, within the bound.
A program may use at most 128 MiB of HBM per device.

```python
import jax
import jax.numpy as jnp
from jax import lax

D = 256
HEADS = 8
HSIZE = 32
DATES = 64
TILES = 4
H = 8
WIDTH = 8


def draw_tokens(key, part):
    shape = (TILES, H, WIDTH, DATES, D)
    first = jax.random.fold_in(jax.random.fold_in(key, 17), 0)
    return jnp.clip(jax.random.normal(first, shape, jnp.float32), -6.0, 6.0).astype(jnp.bfloat16)


def draw_cloud_mask(key, part):
    first, second = jax.random.split(jax.random.fold_in(key, 29), 2)
    clear = jax.random.randint(first, (TILES, H, WIDTH, DATES), 0, 4) != 0
    covered = jax.random.randint(second, (TILES, H, WIDTH), 0, 16) == 0
    return (clear & jnp.logical_not(covered)[..., None]).astype(jnp.int32)


def plant(result, stream_key, least, top_value):
    longest = result.shape.index(max(result.shape))
    spots = []
    for shift in (0, 1):
        where = [jax.random.randint(jax.random.fold_in(stream_key, axis), (), 0, length) for axis, length in enumerate(result.shape)]
        where[longest] = (where[longest] + shift) % result.shape[longest]
        spots.append(tuple(where))
    return result.at[spots[0]].set(least).at[spots[1]].set(top_value)


def steps_of(rng, extent, cuts, smallest, high):
    gain = 1.0
    for dim, shards_of in cuts:
        draws = jax.random.uniform(jax.random.fold_in(jax.random.fold_in(rng, 6), dim), (shards_of,), jnp.float32, smallest / len(cuts), high / len(cuts))
        gain = gain * jnp.repeat(jnp.exp(draws), extent[dim] // shards_of).reshape((-1,) + (1,) * (len(extent) - 1 - dim))
    return gain


def bell_draw(own_key, extent, spread, most, cuts=(), kind=jnp.bfloat16):
    drawn = jax.random.normal(own_key, extent, jnp.float32) * spread
    if len(cuts) > 0:
        drawn = steps_of(own_key, extent, cuts, -0.22, 0.18) * drawn
    return jnp.clip(drawn, min=-most, max=most).astype(kind)


def setup_inputs(seed: int = 0, part: int = 0) -> dict:
    splits = jax.random.split(jax.random.key(seed), 9)
    part_keys = jax.random.split(jax.random.fold_in(splits[8], part), 9)
    tokens = draw_tokens(jax.random.fold_in(jax.random.fold_in(splits[8], part), 71), part)
    cloud_mask = draw_cloud_mask(jax.random.fold_in(jax.random.fold_in(splits[8], part), 71), part)
    day_of_year = plant(jax.random.randint(part_keys[2], (DATES,), 0, 1461), jax.random.fold_in(part_keys[2], 1), 0, 1460).astype(jnp.int32)
    query = bell_draw(splits[3], (D,), 1.5, 6.0, ((0, 2),), jnp.float32)
    key_weight = bell_draw(splits[4], (D, D), D ** -0.5, 0.375, ((1, 2),))
    value_weight = bell_draw(splits[5], (D, D), D ** -0.5, 0.375, ((1, 2),))
    conv_first = bell_draw(splits[6], (3, 3, D, D), D ** -0.5, 0.375, ((3, 2),))
    conv_second = bell_draw(splits[7], (3, 3, D, D), (4 * D) ** -0.5, 0.1875, ((3, 2),))
    return dict(tokens=tokens, cloud_mask=cloud_mask, day_of_year=day_of_year, query=query, key_weight=key_weight, value_weight=value_weight, conv_first=conv_first, conv_second=conv_second)


cloud_penalty = 6.0

def encoding(day_of_year, width):
    chan = jnp.arange(width)
    expo = (2 * (chan // 2)).astype(jnp.float32) / width
    freq = jnp.power(jnp.float32(1000.0), -expo)
    angle = day_of_year.astype(jnp.float32)[:, None] * freq[None, :]
    return jnp.where((chan % 2 == 0)[None, :], jnp.sin(angle), jnp.cos(angle))

def convolve(field, kernel):
    rows, cols = (field.shape[1], field.shape[2])
    padded = jnp.pad(field, ((0, 0), (1, 1), (1, 1), (0, 0)))
    total = jnp.zeros((field.shape[0] * rows * cols, kernel.shape[3]), jnp.float32)
    for arow in range(3):
        for bcol in range(3):
            piece = padded[:, arow:arow + rows, bcol:bcol + cols, :].reshape(-1, field.shape[3])
            total = total + jnp.dot(piece, kernel[arow, bcol], preferred_element_type=jnp.float32)
    return total.reshape(field.shape[0], rows, cols, kernel.shape[3])

def reference(tokens, cloud_mask, day_of_year, query, key_weight, value_weight, conv_first, conv_second):
    table = encoding(day_of_year, D)
    query_heads = query.astype(jnp.float32).reshape(HEADS, HSIZE)

    def one_tile(pair):
        feats, clear = pair
        inputs = (feats.astype(jnp.float32) + table[None, None]).astype(jnp.bfloat16).reshape(-1, D)
        keys = jnp.dot(inputs, key_weight, preferred_element_type=jnp.float32).reshape(H * WIDTH, DATES, HEADS, HSIZE)
        vals = jnp.dot(inputs, value_weight, preferred_element_type=jnp.float32).reshape(H * WIDTH, DATES, HEADS, HSIZE)
        score = lax.optimization_barrier(jnp.sum(keys * query_heads[None, None], axis=-1)) / jnp.sqrt(jnp.float32(HSIZE))
        score = score - cloud_penalty * (1.0 - clear.reshape(H * WIDTH, DATES, 1).astype(jnp.float32))
        attn = jax.nn.softmax(score, axis=1)
        pooled = lax.optimization_barrier(jnp.sum(attn[..., None] * vals, axis=1))
        return pooled.reshape(H, WIDTH, D).astype(jnp.bfloat16)
    pooled = lax.map(one_tile, (tokens, cloud_mask))
    hidden = jax.nn.relu(convolve(pooled, conv_first)).astype(jnp.bfloat16)
    return convolve(hidden, conv_second).astype(jnp.bfloat16)
```

```python
import functools
import math

import jax
import jax.numpy as jnp
from jax import lax
from jax.experimental import pallas as pl
from jax.experimental.pallas import tpu as pltpu
from jax.sharding import PartitionSpec as P

HSIZE = 32
HALO = 2
MESH = pl.DeviceIdType.MESH
F32, BF16 = jnp.float32, jnp.bfloat16


cloud_penalty = 6.0


def iota(shape, dim):
    return lax.broadcasted_iota(jnp.int32, shape, dim)


def frequencies(width):
    pair = iota((1, width), 1) // 2
    freq = jnp.ones((1, width), F32)
    bit = 1
    while bit < width // 2:
        freq = jnp.where((pair // bit) % 2 == 1, freq * F32(1000.0 ** (-2.0 * bit / width)), freq)
        bit *= 2
    return freq


def encoding(days, width):
    angle = days * frequencies(width)
    turns = jnp.floor(angle * F32(2.0 / math.pi) + F32(0.5))
    rest = angle - turns * F32(1.5703125)
    rest = rest - turns * F32(4.837512969970703125e-4)
    rest = rest - turns * F32(7.54978995489188216e-8)
    square = rest * rest
    sine = (F32(-1.9515295891e-4) * square + F32(8.3321608736e-3)) * square + F32(-1.6666654611e-1)
    sine = sine * square * rest + rest
    cosine = (F32(2.443315711809948e-5) * square + F32(-1.388731625493765e-3)) * square
    cosine = (cosine + F32(4.166664568298827e-2)) * square * square - F32(0.5) * square + F32(1.0)
    quadrant = turns.astype(jnp.int32) + iota(angle.shape, 1) % 2
    value = jnp.where(quadrant % 2 == 1, cosine, sine)
    return jnp.where((quadrant // 2) % 2 == 1, -value, value)


def split(value, parts):
    terms = []
    for _ in range(parts):
        term = value.astype(BF16)
        terms.append(term)
        value = value - term.astype(F32)
    return terms


def shifted(field, cols):
    count = field.shape[0]
    col = iota(field.shape, 0) % cols
    left = jnp.where(col == 0, 0.0, pltpu.roll(field, 1, 0))
    right = jnp.where(col == cols - 1, 0.0, pltpu.roll(field, count - 1, 0))
    return left, field, right


def windows(field, cols):
    sides = shifted(field, cols)
    count = field.shape[0] - 2 * cols
    return jnp.concatenate(
        [side[arow * cols : arow * cols + count].astype(BF16) for arow in range(3) for side in sides],
        axis=1,
    )


def kernel(
    sizes,
    tokens,
    mask,
    days,
    query,
    key_weight,
    value_weight,
    conv_first,
    conv_second,
    out,
    tok_v,
    mask_v,
    wk_v,
    wv_v,
    w1_v,
    w2_v,
    proj_v,
    enc_v,
    part_s,
    part_r,
    pool_v,
    tok_sem,
    in_sem,
    w1_send,
    w1_recv,
    part_send,
    part_recv,
    pool_send,
    pool_recv,
):
    n, slabs, rows, cols, dates, width = sizes
    pixels = rows * cols
    chans = query.shape[1]
    date, slab, head = lax.axis_index("date"), lax.axis_index("tile"), lax.axis_index("head")
    other = 1 - head
    has_up, has_down = slab > 0, slab < slabs - 1

    def tile_at(step):
        return lax.rem(date + 1 + step, n)

    def tok_copy(tile):
        return pltpu.make_async_copy(tokens.at[tile], tok_v.at[tile], tok_sem.at[tile])

    loads = [
        pltpu.make_async_copy(key_weight, wk_v, in_sem.at[0]),
        pltpu.make_async_copy(value_weight, wv_v, in_sem.at[1]),
        pltpu.make_async_copy(mask, mask_v, in_sem.at[2]),
        pltpu.make_async_copy(conv_first, w1_v.at[head], in_sem.at[3]),
        pltpu.make_async_copy(conv_second, w2_v, in_sem.at[4]),
    ]
    for load in loads[:3]:
        load.start()

    @pl.loop(0, n)
    def _(step):
        tok_copy(tile_at(step)).start()

    for load in loads[3:]:
        load.start()

    barrier = pltpu.get_barrier_semaphore()

    @pl.loop(1, n)
    def _(step):
        pl.semaphore_signal(barrier, inc=1, device_id={"date": lax.rem(date + step, n)}, device_id_type=MESH)

    pl.semaphore_signal(barrier, inc=1, device_id={"head": other}, device_id_type=MESH)
    for has, off in ((has_up, -1), (has_down, 1)):

        @pl.when(has)
        def _(off=off):
            for core in range(2):
                pl.semaphore_signal(
                    barrier, inc=1, device_id={"tile": slab + off, "head": core}, device_id_type=MESH
                )

    day_row = days[...].astype(F32)
    eye = iota((dates, dates), 0) == iota((dates, dates), 1)
    day_col = jnp.sum(jnp.where(eye, jnp.broadcast_to(day_row, (dates, dates)), 0.0), axis=1, keepdims=True)
    enc_v[...] = encoding(day_col, width)

    same_head = iota((chans, chans), 0) // HSIZE == iota((chans, chans), 1) // HSIZE
    blocks = jnp.where(same_head, 1.0, 0.0).astype(BF16)
    loads[0].wait()
    loads[1].wait()
    scaled = wk_v[...].astype(F32) * (query[...] * F32(1.0 / math.sqrt(HSIZE)))
    folded = jnp.zeros((width, chans), F32)
    for term in split(scaled, 3):
        folded = folded + jnp.dot(term, blocks, preferred_element_type=F32)
    high, low = split(folded, 2)
    proj_v[:, :chans] = wv_v[...]
    proj_v[:, chans : 2 * chans] = high
    proj_v[:, 2 * chans :] = low
    loads[2].wait()

    has_count = has_up.astype(jnp.int32) + has_down.astype(jnp.int32)
    pl.semaphore_wait(barrier, n + 2 * has_count)

    w1_copy = pltpu.make_async_remote_copy(
        src_ref=conv_first,
        dst_ref=w1_v.at[head],
        send_sem=w1_send,
        recv_sem=w1_recv,
        device_id={"head": other},
        device_id_type=MESH,
    )
    w1_copy.start()

    lane = iota((8, chans), 1) % HSIZE // 4
    ones = jnp.ones((dates, chans), BF16)

    def part_copy(tile, slot):
        return pltpu.make_async_remote_copy(
            src_ref=part_s.at[tile],
            dst_ref=part_r.at[slot],
            send_sem=part_send.at[tile],
            recv_sem=part_recv.at[slot],
            device_id={"date": tile},
            device_id_type=MESH,
        )

    def attend(tile):
        feats = tok_v[tile].astype(F32).reshape(pixels, dates, width)
        inputs = (feats + enc_v[...][None]).astype(BF16).reshape(pixels * dates, width)
        both = jnp.dot(inputs, proj_v[...], preferred_element_type=F32)
        clear = jnp.broadcast_to(mask_v[tile].astype(F32)[:, None, :], (pixels, dates, dates))
        cloud = jnp.where(eye[None], F32(-cloud_penalty) * (1.0 - clear), 0.0).astype(BF16)
        cloud = jnp.dot(cloud.reshape(pixels * dates, dates), ones, preferred_element_type=F32)
        score = both[:, chans : 2 * chans] + both[:, 2 * chans :] + cloud
        score = score.reshape(pixels, dates, chans)
        vals = both[:, :chans].reshape(pixels, dates, chans)
        top = jnp.max(score, axis=1)
        expo = jnp.exp(score - top[:, None, :])
        total = jnp.sum(expo, axis=1)
        sums = jnp.sum(expo * vals, axis=1)
        groups = pixels // 8
        stats = top[:8]
        for group in range(groups):
            stats = jnp.where(lane == group, top[group * 8 : group * 8 + 8], stats)
            stats = jnp.where(lane == group + groups, total[group * 8 : group * 8 + 8], stats)
        return sums, stats

    @pl.loop(0, n - 1)
    def _(step):
        tile = tile_at(step)
        tok_copy(tile).wait()
        sums, stats = attend(tile)
        part_s[tile, :pixels] = sums
        part_s[tile, pixels:] = stats
        part_copy(tile, date).start()

    tok_copy(date).wait()
    sums, stats = attend(date)
    part_r[date, :pixels] = sums
    part_r[date, pixels:] = stats

    @pl.loop(1, n)
    def _(step):
        part_copy(date, lax.rem(date + step, n)).wait_recv()

    best = part_r[0, pixels:]
    for source in range(1, n):
        best = jnp.maximum(best, part_r[source, pixels:])
    scales = []
    tots = jnp.zeros((8, chans), F32)
    for source in range(n):
        stat = part_r[source, pixels:]
        scale = jnp.exp(stat - best)
        scales.append(scale)
        tots = tots + scale * pltpu.roll(stat, chans - HSIZE // 2, 1)
    inverse = 1.0 / tots
    groups = pixels // 8
    pooled = [jnp.zeros((8, chans), F32) for _ in range(groups)]
    for source in range(n):
        weight = scales[source] * inverse
        for group in range(groups):
            wide = weight if group == 0 else pltpu.roll(weight, chans - 4 * group, 1)
            wide = jnp.where(lane == 0, wide, 0.0)
            for step in (4, 8, 16):
                wide = wide + pltpu.roll(wide, step, 1)
            pooled[group] = pooled[group] + wide * part_r[source, group * 8 : group * 8 + 8]
    halo = HALO * cols
    pool_v[head, halo : halo + pixels] = jnp.concatenate(pooled, axis=0).astype(BF16)

    def pool_copy(index, source, target, count, where):
        return pltpu.make_async_remote_copy(
            src_ref=pool_v.at[head, pl.ds(source, count)],
            dst_ref=pool_v.at[head, pl.ds(target, count)],
            send_sem=pool_send.at[index],
            recv_sem=pool_recv.at[index],
            device_id=where,
            device_id_type=MESH,
        )

    def sends(fn):
        fn(pool_copy(0, halo, halo, pixels, {"head": other}))

        @pl.when(has_up)
        def _():
            for hop in range(2):
                core = other if hop == 0 else head
                fn(pool_copy(1 + hop, halo, halo + pixels, halo, {"tile": slab - 1, "head": core}))

        @pl.when(has_down)
        def _():
            for hop in range(2):
                core = other if hop == 0 else head
                fn(pool_copy(3 + hop, pixels, 0, halo, {"tile": slab + 1, "head": core}))

    sends(lambda copy: copy.start())

    zeros = jnp.zeros((2, halo, chans), BF16)

    @pl.when(jnp.logical_not(has_up))
    def _():
        pool_v[:, :halo] = zeros

    @pl.when(jnp.logical_not(has_down))
    def _():
        pool_v[:, halo + pixels :] = zeros

    for load in loads[3:]:
        load.wait()
    w1_copy.wait()

    pool_copy(0, halo, halo, pixels, {"head": other}).wait_recv()

    @pl.when(has_down)
    def _():
        for hop in range(2):
            pool_copy(1 + hop, halo, halo + pixels, halo, {"head": other}).wait_recv()

    @pl.when(has_up)
    def _():
        for hop in range(2):
            pool_copy(3 + hop, pixels, 0, halo, {"head": other}).wait_recv()

    field = jnp.concatenate([pool_v[0], pool_v[1]], axis=1).astype(F32)
    first = jnp.concatenate([w1_v[0], w1_v[1]], axis=1)
    hidden = jnp.dot(windows(field, cols), first, preferred_element_type=F32)
    hidden = jnp.maximum(hidden, 0.0).astype(BF16).astype(F32)
    place = iota(hidden.shape, 0) // cols + (slab * rows - 1)
    hidden = jnp.where((place >= 0) & (place < slabs * rows), hidden, 0.0)
    out[...] = jnp.dot(windows(hidden, cols), w2_v[...], preferred_element_type=F32).astype(BF16)

    @pl.loop(0, n - 1)
    def _(step):
        part_copy(tile_at(step), date).wait_send()

    sends(lambda copy: copy.wait_send())


def local(n, slabs, tokens, cloud_mask, day_of_year, query, key_weight, value_weight, conv_first, conv_second):
    tiles, rows, cols, dates, width = tokens.shape
    pixels = rows * cols
    chans = query.shape[0]
    depth = 9 * width
    anywhere = pl.BlockSpec(memory_space=pl.ANY)
    vmem = pl.BlockSpec(memory_space=pltpu.VMEM)
    result = pl.pallas_call(
        functools.partial(kernel, (n, slabs, rows, cols, dates, width)),
        out_shape=jax.ShapeDtypeStruct((pixels, chans), BF16),
        in_specs=[anywhere, anywhere, vmem, vmem] + [anywhere] * 4,
        out_specs=vmem,
        scratch_shapes=[
            pltpu.VMEM((n, pixels * dates, width), BF16),
            pltpu.VMEM((n, pixels, dates), jnp.int32),
            pltpu.VMEM((width, chans), BF16),
            pltpu.VMEM((width, chans), BF16),
            pltpu.VMEM((2, depth, chans), BF16),
            pltpu.VMEM((depth, chans), BF16),
            pltpu.VMEM((width, 3 * chans), BF16),
            pltpu.VMEM((dates, width), F32),
            pltpu.VMEM((n, pixels + 8, chans), F32),
            pltpu.VMEM((n, pixels + 8, chans), F32),
            pltpu.VMEM((2, pixels + 2 * HALO * cols, chans), BF16),
            pltpu.SemaphoreType.DMA((n,)),
            pltpu.SemaphoreType.DMA((5,)),
            pltpu.SemaphoreType.DMA,
            pltpu.SemaphoreType.DMA,
            pltpu.SemaphoreType.DMA((n,)),
            pltpu.SemaphoreType.DMA((n,)),
            pltpu.SemaphoreType.DMA((5,)),
            pltpu.SemaphoreType.DMA((5,)),
        ],
        compiler_params=pltpu.CompilerParams(
            collective_id=0, has_side_effects=True, vmem_limit_bytes=48 * 1024 * 1024
        ),
    )(
        tokens.reshape(tiles, pixels * dates, width),
        cloud_mask.reshape(tiles, pixels, dates),
        day_of_year.reshape(1, dates),
        query.reshape(1, chans),
        key_weight,
        value_weight,
        conv_first.reshape(depth, chans),
        conv_second.reshape(depth, chans),
    )
    return result.reshape(1, rows, cols, chans)


def solution(mesh):
    in_specs = (
        P("groups", "tile", None, "date", None),
        P("groups", "tile", None, "date"),
        P(("groups", "date")),
        P("head"),
        P(None, "head"),
        P(None, "head"),
        P(None, None, None, "head"),
        P(None, None, None, "head"),
    )
    out_specs = P(("groups", "date"), "tile", None, "head")
    body = functools.partial(local, mesh.shape["date"], mesh.shape["tile"])
    return jax.shard_map(body, mesh=mesh, in_specs=in_specs, out_specs=out_specs, check_vma=False)
```

```python
import functools
import math

import jax
import jax.numpy as jnp
from jax import lax
from jax.experimental import pallas as pl
from jax.experimental.pallas import tpu as pltpu
from jax.sharding import PartitionSpec as P

HSIZE = 32
HALO = 2
MESH = pl.DeviceIdType.MESH
F32, BF16 = jnp.float32, jnp.bfloat16


cloud_penalty = 6.0


def iota(shape, dim):
    return lax.broadcasted_iota(jnp.int32, shape, dim)


def frequencies(width):
    pair = iota((1, width), 1) // 2
    freq = jnp.ones((1, width), F32)
    bit = 1
    while bit < width // 2:
        freq = jnp.where((pair // bit) % 2 == 1, freq * F32(1000.0 ** (-2.0 * bit / width)), freq)
        bit *= 2
    return freq


def encoding(days, width):
    angle = days * frequencies(width)
    turns = jnp.floor(angle * F32(2.0 / math.pi) + F32(0.5))
    rest = angle - turns * F32(1.5703125)
    rest = rest - turns * F32(4.837512969970703125e-4)
    rest = rest - turns * F32(7.54978995489188216e-8)
    square = rest * rest
    sine = (F32(-1.9515295891e-4) * square + F32(8.3321608736e-3)) * square + F32(-1.6666654611e-1)
    sine = sine * square * rest + rest
    cosine = (F32(2.443315711809948e-5) * square + F32(-1.388731625493765e-3)) * square
    cosine = (cosine + F32(4.166664568298827e-2)) * square * square - F32(0.5) * square + F32(1.0)
    quadrant = turns.astype(jnp.int32) + iota(angle.shape, 1) % 2
    value = jnp.where(quadrant % 2 == 1, cosine, sine)
    return jnp.where((quadrant // 2) % 2 == 1, -value, value)


def split(value, parts):
    terms = []
    for _ in range(parts):
        term = value.astype(BF16)
        terms.append(term)
        value = value - term.astype(F32)
    return terms


def shifted(field, cols):
    count = field.shape[0]
    col = iota(field.shape, 0) % cols
    left = jnp.where(col == 0, 0.0, pltpu.roll(field, 1, 0))
    right = jnp.where(col == cols - 1, 0.0, pltpu.roll(field, count - 1, 0))
    return left, field, right


def windows(field, cols):
    sides = shifted(field, cols)
    count = field.shape[0] - 2 * cols
    return jnp.concatenate(
        [side[arow * cols : arow * cols + count].astype(BF16) for arow in range(3) for side in sides],
        axis=1,
    )


def kernel(
    sizes,
    tokens,
    mask,
    days,
    query,
    key_weight,
    value_weight,
    conv_first,
    conv_second,
    out,
    tok_v,
    mask_v,
    days_v,
    query_v,
    wk_v,
    wv_v,
    w1_v,
    w2_v,
    proj_v,
    enc_v,
    part_s,
    part_r,
    pool_v,
    tok_sem,
    in_sem,
    w1_send,
    w1_recv,
    part_send,
    part_recv,
    pool_send,
    pool_recv,
):
    n, slabs, rows, cols, dates, width = sizes
    pixels = rows * cols
    chans = query.shape[1]
    date, slab, head = lax.axis_index("date"), lax.axis_index("tile"), lax.axis_index("head")
    other = 1 - head
    has_up, has_down = slab > 0, slab < slabs - 1

    def tile_at(step):
        return lax.rem(date + 1 + step, n)

    def tok_copy(tile):
        return pltpu.make_async_copy(tokens.at[tile], tok_v.at[tile], tok_sem.at[tile])

    loads = [
        pltpu.make_async_copy(days, days_v, in_sem.at[0]),
        pltpu.make_async_copy(query, query_v, in_sem.at[1]),
        pltpu.make_async_copy(key_weight, wk_v, in_sem.at[2]),
        pltpu.make_async_copy(value_weight, wv_v, in_sem.at[3]),
        pltpu.make_async_copy(mask, mask_v, in_sem.at[4]),
        pltpu.make_async_copy(conv_first, w1_v.at[head], in_sem.at[5]),
        pltpu.make_async_copy(conv_second, w2_v, in_sem.at[6]),
    ]
    for load in loads[:5]:
        load.start()

    @pl.loop(0, n)
    def _(step):
        tok_copy(tile_at(step)).start()

    for load in loads[5:]:
        load.start()

    barrier = pltpu.get_barrier_semaphore()

    @pl.loop(1, n)
    def _(step):
        pl.semaphore_signal(barrier, inc=1, device_id={"date": lax.rem(date + step, n)}, device_id_type=MESH)

    pl.semaphore_signal(barrier, inc=1, device_id={"head": other}, device_id_type=MESH)
    for has, off in ((has_up, -1), (has_down, 1)):

        @pl.when(has)
        def _(off=off):
            for core in range(2):
                pl.semaphore_signal(
                    barrier, inc=1, device_id={"tile": slab + off, "head": core}, device_id_type=MESH
                )

    loads[0].wait()
    day_row = days_v[...].astype(F32)
    eye = iota((dates, dates), 0) == iota((dates, dates), 1)
    day_col = jnp.sum(jnp.where(eye, jnp.broadcast_to(day_row, (dates, dates)), 0.0), axis=1, keepdims=True)
    enc_v[...] = encoding(day_col, width)

    same_head = iota((chans, chans), 0) // HSIZE == iota((chans, chans), 1) // HSIZE
    blocks = jnp.where(same_head, 1.0, 0.0).astype(BF16)
    for load in loads[1:4]:
        load.wait()
    scaled = wk_v[...].astype(F32) * (query_v[...] * F32(1.0 / math.sqrt(HSIZE)))
    folded = jnp.zeros((width, chans), F32)
    for term in split(scaled, 3):
        folded = folded + jnp.dot(term, blocks, preferred_element_type=F32)
    high, low = split(folded, 2)
    proj_v[:, :chans] = wv_v[...]
    proj_v[:, chans : 2 * chans] = high
    proj_v[:, 2 * chans :] = low
    loads[4].wait()

    has_count = has_up.astype(jnp.int32) + has_down.astype(jnp.int32)
    pl.semaphore_wait(barrier, n + 2 * has_count)

    w1_copy = pltpu.make_async_remote_copy(
        src_ref=conv_first,
        dst_ref=w1_v.at[head],
        send_sem=w1_send,
        recv_sem=w1_recv,
        device_id={"head": other},
        device_id_type=MESH,
    )
    w1_copy.start()

    lane = iota((8, chans), 1) % HSIZE // 4
    ones = jnp.ones((dates, chans), BF16)

    def part_copy(tile, slot):
        return pltpu.make_async_remote_copy(
            src_ref=part_s.at[tile],
            dst_ref=part_r.at[slot],
            send_sem=part_send.at[tile],
            recv_sem=part_recv.at[slot],
            device_id={"date": tile},
            device_id_type=MESH,
        )

    def attend(tile):
        feats = tok_v[tile].astype(F32).reshape(pixels, dates, width)
        inputs = (feats + enc_v[...][None]).astype(BF16).reshape(pixels * dates, width)
        both = jnp.dot(inputs, proj_v[...], preferred_element_type=F32)
        clear = jnp.broadcast_to(mask_v[tile].astype(F32)[:, None, :], (pixels, dates, dates))
        cloud = jnp.where(eye[None], F32(-cloud_penalty) * (1.0 - clear), 0.0).astype(BF16)
        cloud = jnp.dot(cloud.reshape(pixels * dates, dates), ones, preferred_element_type=F32)
        score = both[:, chans : 2 * chans] + both[:, 2 * chans :] + cloud
        score = score.reshape(pixels, dates, chans)
        vals = both[:, :chans].reshape(pixels, dates, chans)
        top = jnp.max(score, axis=1)
        expo = jnp.exp(score - top[:, None, :])
        total = jnp.sum(expo, axis=1)
        sums = jnp.sum(expo * vals, axis=1)
        groups = pixels // 8
        stats = top[:8]
        for group in range(groups):
            stats = jnp.where(lane == group, top[group * 8 : group * 8 + 8], stats)
            stats = jnp.where(lane == group + groups, total[group * 8 : group * 8 + 8], stats)
        return sums, stats

    @pl.loop(0, n - 1)
    def _(step):
        tile = tile_at(step)
        tok_copy(tile).wait()
        sums, stats = attend(tile)
        part_s[tile, :pixels] = sums
        part_s[tile, pixels:] = stats
        part_copy(tile, date).start()

    tok_copy(date).wait()
    sums, stats = attend(date)
    part_r[date, :pixels] = sums
    part_r[date, pixels:] = stats

    @pl.loop(1, n)
    def _(step):
        part_copy(date, lax.rem(date + step, n)).wait_recv()

    best = part_r[0, pixels:]
    for source in range(1, n):
        best = jnp.maximum(best, part_r[source, pixels:])
    scales = []
    tots = jnp.zeros((8, chans), F32)
    for source in range(n):
        stat = part_r[source, pixels:]
        scale = jnp.exp(stat - best)
        scales.append(scale)
        tots = tots + scale * pltpu.roll(stat, chans - HSIZE // 2, 1)
    inverse = 1.0 / tots
    groups = pixels // 8
    pooled = [jnp.zeros((8, chans), F32) for _ in range(groups)]
    for source in range(n):
        weight = scales[source] * inverse
        for group in range(groups):
            wide = weight if group == 0 else pltpu.roll(weight, chans - 4 * group, 1)
            wide = jnp.where(lane == 0, wide, 0.0)
            for step in (4, 8, 16):
                wide = wide + pltpu.roll(wide, step, 1)
            pooled[group] = pooled[group] + wide * part_r[source, group * 8 : group * 8 + 8]
    halo = HALO * cols
    pool_v[head, halo : halo + pixels] = jnp.concatenate(pooled, axis=0).astype(BF16)

    def pool_copy(index, source, target, count, where):
        return pltpu.make_async_remote_copy(
            src_ref=pool_v.at[head, pl.ds(source, count)],
            dst_ref=pool_v.at[head, pl.ds(target, count)],
            send_sem=pool_send.at[index],
            recv_sem=pool_recv.at[index],
            device_id=where,
            device_id_type=MESH,
        )

    def sends(fn):
        fn(pool_copy(0, halo, halo, pixels, {"head": other}))

        @pl.when(has_up)
        def _():
            for hop in range(2):
                core = other if hop == 0 else head
                fn(pool_copy(1 + hop, halo, halo + pixels, halo, {"tile": slab - 1, "head": core}))

        @pl.when(has_down)
        def _():
            for hop in range(2):
                core = other if hop == 0 else head
                fn(pool_copy(3 + hop, pixels, 0, halo, {"tile": slab + 1, "head": core}))

    sends(lambda copy: copy.start())

    zeros = jnp.zeros((2, halo, chans), BF16)

    @pl.when(jnp.logical_not(has_up))
    def _():
        pool_v[:, :halo] = zeros

    @pl.when(jnp.logical_not(has_down))
    def _():
        pool_v[:, halo + pixels :] = zeros

    for load in loads[5:]:
        load.wait()
    w1_copy.wait()

    pool_copy(0, halo, halo, pixels, {"head": other}).wait_recv()

    @pl.when(has_down)
    def _():
        for hop in range(2):
            pool_copy(1 + hop, halo, halo + pixels, halo, {"head": other}).wait_recv()

    @pl.when(has_up)
    def _():
        for hop in range(2):
            pool_copy(3 + hop, pixels, 0, halo, {"head": other}).wait_recv()

    field = jnp.concatenate([pool_v[0], pool_v[1]], axis=1).astype(F32)
    first = jnp.concatenate([w1_v[0], w1_v[1]], axis=1)
    hidden = jnp.dot(windows(field, cols), first, preferred_element_type=F32)
    hidden = jnp.maximum(hidden, 0.0).astype(BF16).astype(F32)
    place = iota(hidden.shape, 0) // cols + (slab * rows - 1)
    hidden = jnp.where((place >= 0) & (place < slabs * rows), hidden, 0.0)
    out[...] = jnp.dot(windows(hidden, cols), w2_v[...], preferred_element_type=F32).astype(BF16)

    @pl.loop(0, n - 1)
    def _(step):
        part_copy(tile_at(step), date).wait_send()

    sends(lambda copy: copy.wait_send())


def local(n, slabs, tokens, cloud_mask, day_of_year, query, key_weight, value_weight, conv_first, conv_second):
    tiles, rows, cols, dates, width = tokens.shape
    pixels = rows * cols
    chans = query.shape[0]
    depth = 9 * width
    hbm = pl.BlockSpec(memory_space=pltpu.HBM)
    vmem = pl.BlockSpec(memory_space=pltpu.VMEM)
    result = pl.pallas_call(
        functools.partial(kernel, (n, slabs, rows, cols, dates, width)),
        out_shape=jax.ShapeDtypeStruct((pixels, chans), BF16),
        in_specs=[hbm] * 8,
        out_specs=vmem,
        scratch_shapes=[
            pltpu.VMEM((n, pixels * dates, width), BF16),
            pltpu.VMEM((n, pixels, dates), jnp.int32),
            pltpu.VMEM((1, dates), jnp.int32),
            pltpu.VMEM((1, chans), F32),
            pltpu.VMEM((width, chans), BF16),
            pltpu.VMEM((width, chans), BF16),
            pltpu.VMEM((2, depth, chans), BF16),
            pltpu.VMEM((depth, chans), BF16),
            pltpu.VMEM((width, 3 * chans), BF16),
            pltpu.VMEM((dates, width), F32),
            pltpu.VMEM((n, pixels + 8, chans), F32),
            pltpu.VMEM((n, pixels + 8, chans), F32),
            pltpu.VMEM((2, pixels + 2 * HALO * cols, chans), BF16),
            pltpu.SemaphoreType.DMA((n,)),
            pltpu.SemaphoreType.DMA((7,)),
            pltpu.SemaphoreType.DMA,
            pltpu.SemaphoreType.DMA,
            pltpu.SemaphoreType.DMA((n,)),
            pltpu.SemaphoreType.DMA((n,)),
            pltpu.SemaphoreType.DMA((5,)),
            pltpu.SemaphoreType.DMA((5,)),
        ],
        compiler_params=pltpu.CompilerParams(
            collective_id=0, has_side_effects=True, vmem_limit_bytes=48 * 1024 * 1024
        ),
    )(
        tokens.reshape(tiles, pixels * dates, width),
        cloud_mask.reshape(tiles, pixels, dates),
        day_of_year.reshape(1, dates),
        query.reshape(1, chans),
        key_weight,
        value_weight,
        conv_first.reshape(depth, chans),
        conv_second.reshape(depth, chans),
    )
    return result.reshape(1, rows, cols, chans)


def solution(mesh):
    in_specs = (
        P("groups", "tile", None, "date", None),
        P("groups", "tile", None, "date"),
        P(("groups", "date")),
        P("head"),
        P(None, "head"),
        P(None, "head"),
        P(None, None, None, "head"),
        P(None, None, None, "head"),
    )
    out_specs = P(("groups", "date"), "tile", None, "head")
    body = functools.partial(local, mesh.shape["date"], mesh.shape["tile"])
    return jax.shard_map(body, mesh=mesh, in_specs=in_specs, out_specs=out_specs, check_vma=False)
```

```python
import functools
import math

import jax
import jax.numpy as jnp
from jax import lax
from jax.experimental import pallas as pl
from jax.experimental.pallas import tpu as pltpu
from jax.sharding import PartitionSpec as P

HSIZE = 32
HALO = 2
MESH = pl.DeviceIdType.MESH
F32, BF16 = jnp.float32, jnp.bfloat16


cloud_penalty = 6.0


def iota(shape, dim):
    return lax.broadcasted_iota(jnp.int32, shape, dim)


def frequencies(width):
    pair = iota((1, width), 1) // 2
    freq = jnp.ones((1, width), F32)
    bit = 1
    while bit < width // 2:
        freq = jnp.where((pair // bit) % 2 == 1, freq * F32(1000.0 ** (-2.0 * bit / width)), freq)
        bit *= 2
    return freq


def encoding(days, width):
    angle = days * frequencies(width)
    turns = jnp.floor(angle * F32(2.0 / math.pi) + F32(0.5))
    rest = angle - turns * F32(1.5703125)
    rest = rest - turns * F32(4.837512969970703125e-4)
    rest = rest - turns * F32(7.54978995489188216e-8)
    square = rest * rest
    sine = (F32(-1.9515295891e-4) * square + F32(8.3321608736e-3)) * square + F32(-1.6666654611e-1)
    sine = sine * square * rest + rest
    cosine = (F32(2.443315711809948e-5) * square + F32(-1.388731625493765e-3)) * square
    cosine = (cosine + F32(4.166664568298827e-2)) * square * square - F32(0.5) * square + F32(1.0)
    quadrant = turns.astype(jnp.int32) + iota(angle.shape, 1) % 2
    value = jnp.where(quadrant % 2 == 1, cosine, sine)
    return jnp.where((quadrant // 2) % 2 == 1, -value, value)


def split(value, parts):
    terms = []
    for _ in range(parts):
        term = value.astype(BF16)
        terms.append(term)
        value = value - term.astype(F32)
    return terms


def shifted(field, cols):
    count = field.shape[0]
    col = iota(field.shape, 0) % cols
    left = jnp.where(col == 0, 0.0, pltpu.roll(field, 1, 0))
    right = jnp.where(col == cols - 1, 0.0, pltpu.roll(field, count - 1, 0))
    return left, field, right


def windows(field, cols):
    sides = shifted(field, cols)
    count = field.shape[0] - 2 * cols
    return jnp.concatenate(
        [side[arow * cols : arow * cols + count].astype(BF16) for arow in range(3) for side in sides],
        axis=1,
    )


def kernel(
    sizes,
    tokens,
    mask,
    days,
    query,
    key_weight,
    value_weight,
    conv_first,
    conv_second,
    out,
    tok_v,
    mask_v,
    days_v,
    query_v,
    wk_v,
    wv_v,
    w1_v,
    w2_v,
    proj_v,
    enc_v,
    part_s,
    part_r,
    low_r,
    high_r,
    pool_v,
    tok_sem,
    in_sem,
    w1_send,
    w1_recv,
    part_send,
    part_recv,
    pool_send,
    pool_recv,
):
    n, slabs, rows, cols, dates, width = sizes
    pixels = rows * cols
    chans = query.shape[1]
    date, slab, head = lax.axis_index("date"), lax.axis_index("tile"), lax.axis_index("head")
    other = 1 - head
    has_up, has_down = slab > 0, slab < slabs - 1

    def tile_at(step):
        return lax.rem(date + 1 + step, n)

    def tok_copy(tile):
        return pltpu.make_async_copy(tokens.at[tile], tok_v.at[tile], tok_sem.at[tile])

    barrier = pltpu.get_barrier_semaphore()

    def signal(where):
        pl.semaphore_signal(barrier, inc=1, device_id=where, device_id_type=MESH)

    @pl.loop(1, n)
    def _(step):
        signal({"date": lax.rem(date + step, n)})

    for has, off in ((has_up, -1), (has_down, 1)):

        @pl.when(has)
        def _(off=off):
            @pl.loop(0, n)
            def _(step):
                signal({"date": lax.rem(date + step, n), "tile": slab + off})

    signal({"head": other})

    loads = [
        pltpu.make_async_copy(days, days_v, in_sem.at[0]),
        pltpu.make_async_copy(query, query_v, in_sem.at[1]),
        pltpu.make_async_copy(key_weight, wk_v, in_sem.at[2]),
        pltpu.make_async_copy(value_weight, wv_v, in_sem.at[3]),
        pltpu.make_async_copy(mask, mask_v, in_sem.at[4]),
        pltpu.make_async_copy(conv_first, w1_v.at[head], in_sem.at[5]),
        pltpu.make_async_copy(conv_second, w2_v, in_sem.at[6]),
    ]
    for load in loads[:5]:
        load.start()

    @pl.loop(0, n)
    def _(step):
        tok_copy(tile_at(step)).start()

    for load in loads[5:]:
        load.start()

    loads[0].wait()
    day_row = days_v[...].astype(F32)
    eye = iota((dates, dates), 0) == iota((dates, dates), 1)
    day_col = jnp.sum(jnp.where(eye, jnp.broadcast_to(day_row, (dates, dates)), 0.0), axis=1, keepdims=True)
    enc_v[...] = encoding(day_col, width)

    same_head = iota((chans, chans), 0) // HSIZE == iota((chans, chans), 1) // HSIZE
    blocks = jnp.where(same_head, 1.0, 0.0).astype(BF16)
    for load in loads[1:4]:
        load.wait()
    scaled = wk_v[...].astype(F32) * (query_v[...] * F32(1.0 / math.sqrt(HSIZE)))
    folded = jnp.zeros((width, chans), F32)
    for term in split(scaled, 3):
        folded = folded + jnp.dot(term, blocks, preferred_element_type=F32)
    high, low = split(folded, 2)
    proj_v[:, :chans] = wv_v[...]
    proj_v[:, chans : 2 * chans] = high
    proj_v[:, 2 * chans :] = low
    loads[4].wait()

    lane = iota((8, chans), 1) % HSIZE // 4
    ones = jnp.ones((dates, chans), BF16)

    halo = HALO * cols
    ends = halo + 16

    def part_copy(way, tile, slot):
        start, count = ((0, pixels + 16), (0, ends), (pixels - halo, ends))[way]
        return pltpu.make_async_remote_copy(
            src_ref=part_s.at[tile, pl.ds(start, count)],
            dst_ref=(part_r, low_r, high_r)[way].at[slot],
            send_sem=part_send.at[way, tile],
            recv_sem=part_recv.at[way, slot],
            device_id=({"date": tile}, {"date": tile, "tile": slab - 1}, {"date": tile, "tile": slab + 1})[way],
            device_id_type=MESH,
        )

    def beside(fn):
        @pl.when(has_up)
        def _():
            fn(1)

        @pl.when(has_down)
        def _():
            fn(2)

    def attend(tile):
        feats = tok_v[tile].astype(F32).reshape(pixels, dates, width)
        inputs = (feats + enc_v[...][None]).astype(BF16).reshape(pixels * dates, width)
        both = jnp.dot(inputs, proj_v[...], preferred_element_type=F32)
        clear = jnp.broadcast_to(mask_v[tile].astype(F32)[:, None, :], (pixels, dates, dates))
        cloud = jnp.where(eye[None], F32(-cloud_penalty) * (1.0 - clear), 0.0).astype(BF16)
        cloud = jnp.dot(cloud.reshape(pixels * dates, dates), ones, preferred_element_type=F32)
        score = both[:, chans : 2 * chans] + both[:, 2 * chans :] + cloud
        score = score.reshape(pixels, dates, chans)
        vals = both[:, :chans].reshape(pixels, dates, chans)
        top = sum(term.astype(F32) for term in split(jnp.max(score, axis=1), 2))
        expo = jnp.exp(score - top[:, None, :])
        total = jnp.sum(expo, axis=1)
        sums = jnp.sum(expo * vals, axis=1)
        groups = pixels // 8
        stats = top[:8]
        for group in range(groups):
            stats = jnp.where(lane == group, top[group * 8 : group * 8 + 8], stats)
            stats = jnp.where(lane == group + groups, total[group * 8 : group * 8 + 8], stats)
        part_s[tile, :halo] = sums[:halo].astype(BF16)
        part_s[tile, halo:ends] = jnp.concatenate(split(stats, 2), axis=0)
        part_s[tile, ends:] = sums[halo:].astype(BF16)

    @pl.loop(0, n - 1)
    def _(step):
        tile = tile_at(step)
        tok_copy(tile).wait()
        attend(tile)

    sides = has_up.astype(jnp.int32) + has_down.astype(jnp.int32)
    pl.semaphore_wait(barrier, n + n * sides)

    @pl.loop(0, n - 1)
    def _(step):
        part_copy(0, tile_at(step), date).start()
        beside(lambda way: part_copy(way, tile_at(step), date).start())

    tok_copy(date).wait()
    attend(date)
    beside(lambda way: part_copy(way, date, date).start())
    w1_copy = pltpu.make_async_remote_copy(
        src_ref=conv_first,
        dst_ref=w1_v.at[head],
        send_sem=w1_send,
        recv_sem=w1_recv,
        device_id={"head": other},
        device_id_type=MESH,
    )
    w1_copy.start()
    part_r[date] = part_s[date]

    groups = pixels // 8

    def merge(parts, at, stat_at, first, count):
        def stat_of(source):
            both = parts[source, stat_at : stat_at + 16].astype(F32)
            return both[:8] + both[8:]

        stats = [stat_of(source) for source in range(n)]
        best = functools.reduce(jnp.maximum, stats)
        scales = [jnp.exp(stat - best) for stat in stats]
        tots = sum(scale * pltpu.roll(stat, chans - HSIZE // 2, 1) for scale, stat in zip(scales, stats))
        inverse = 1.0 / tots
        total = jnp.zeros((8 * count, chans), F32)
        for source in range(n):
            weight = scales[source] * inverse
            wides = []
            for group in range(first, first + count):
                wide = weight if group == 0 else pltpu.roll(weight, chans - 4 * group, 1)
                wide = jnp.where(lane == 0, wide, 0.0)
                for step in (4, 8, 16):
                    wide = wide + pltpu.roll(wide, step, 1)
                wides.append(wide)
            sums = parts[source, at : at + 8 * count].astype(F32)
            total = total + jnp.concatenate(wides, axis=0) * sums
        return total.astype(BF16)

    half = groups // 2

    @pl.when(has_up)
    def _():
        @pl.loop(0, n)
        def _(source):
            part_copy(2, date, source).wait_recv()

        pool_v[head, :halo] = merge(high_r, 16, 0, half, half)

    @pl.when(has_down)
    def _():
        @pl.loop(0, n)
        def _(source):
            part_copy(1, date, source).wait_recv()

        pool_v[head, halo + pixels :] = merge(low_r, 0, halo, 0, half)

    @pl.loop(1, n)
    def _(step):
        part_copy(0, date, lax.rem(date + step, n)).wait_recv()

    zeros = jnp.zeros((halo, chans), BF16)

    @pl.when(jnp.logical_not(has_up))
    def _():
        pool_v[head, :halo] = zeros

    @pl.when(jnp.logical_not(has_down))
    def _():
        pool_v[head, halo + pixels :] = zeros

    pool_v[head, halo : 2 * halo] = merge(part_r, 0, halo, 0, half)
    pool_v[head, 2 * halo : 3 * halo] = merge(part_r, ends, halo, half, half)

    pool_copy = pltpu.make_async_remote_copy(
        src_ref=pool_v.at[head],
        dst_ref=pool_v.at[head],
        send_sem=pool_send,
        recv_sem=pool_recv,
        device_id={"head": other},
        device_id_type=MESH,
    )
    pool_copy.start()
    for load in loads[5:]:
        load.wait()
    w1_copy.wait()
    pool_copy.wait_recv()

    field = jnp.concatenate([pool_v[0], pool_v[1]], axis=1).astype(F32)
    first = jnp.concatenate([w1_v[0], w1_v[1]], axis=1)
    hidden = jnp.dot(windows(field, cols), first, preferred_element_type=F32)
    hidden = jnp.maximum(hidden, 0.0).astype(BF16).astype(F32)
    place = iota(hidden.shape, 0) // cols + (slab * rows - 1)
    hidden = jnp.where((place >= 0) & (place < slabs * rows), hidden, 0.0)
    out[...] = jnp.dot(windows(hidden, cols), w2_v[...], preferred_element_type=F32).astype(BF16)

    @pl.loop(0, n - 1)
    def _(step):
        part_copy(0, tile_at(step), date).wait_send()

    def sent(way):
        @pl.loop(0, n)
        def _(tile):
            part_copy(way, tile, date).wait_send()

    beside(sent)
    pool_copy.wait_send()


def local(n, slabs, tokens, cloud_mask, day_of_year, query, key_weight, value_weight, conv_first, conv_second):
    tiles, rows, cols, dates, width = tokens.shape
    pixels = rows * cols
    chans = query.shape[0]
    depth = 9 * width
    hbm = pl.BlockSpec(memory_space=pltpu.HBM)
    vmem = pl.BlockSpec(memory_space=pltpu.VMEM)
    result = pl.pallas_call(
        functools.partial(kernel, (n, slabs, rows, cols, dates, width)),
        out_shape=jax.ShapeDtypeStruct((pixels, chans), BF16),
        in_specs=[hbm] * 8,
        out_specs=vmem,
        scratch_shapes=[
            pltpu.VMEM((n, pixels * dates, width), BF16),
            pltpu.VMEM((n, pixels, dates), jnp.int32),
            pltpu.VMEM((1, dates), jnp.int32),
            pltpu.VMEM((1, chans), F32),
            pltpu.VMEM((width, chans), BF16),
            pltpu.VMEM((width, chans), BF16),
            pltpu.VMEM((2, depth, chans), BF16),
            pltpu.VMEM((depth, chans), BF16),
            pltpu.VMEM((width, 3 * chans), BF16),
            pltpu.VMEM((dates, width), F32),
            pltpu.VMEM((n, pixels + 16, chans), BF16),
            pltpu.VMEM((n, pixels + 16, chans), BF16),
            pltpu.VMEM((n, HALO * cols + 16, chans), BF16),
            pltpu.VMEM((n, HALO * cols + 16, chans), BF16),
            pltpu.VMEM((2, pixels + 2 * HALO * cols, chans), BF16),
            pltpu.SemaphoreType.DMA((n,)),
            pltpu.SemaphoreType.DMA((7,)),
            pltpu.SemaphoreType.DMA,
            pltpu.SemaphoreType.DMA,
            pltpu.SemaphoreType.DMA((3, n)),
            pltpu.SemaphoreType.DMA((3, n)),
            pltpu.SemaphoreType.DMA,
            pltpu.SemaphoreType.DMA,
        ],
        compiler_params=pltpu.CompilerParams(
            collective_id=0, has_side_effects=True, vmem_limit_bytes=60 * 1024 * 1024
        ),
    )(
        tokens.reshape(tiles, pixels * dates, width),
        cloud_mask.reshape(tiles, pixels, dates),
        day_of_year.reshape(1, dates),
        query.reshape(1, chans),
        key_weight,
        value_weight,
        conv_first.reshape(depth, chans),
        conv_second.reshape(depth, chans),
    )
    return result.reshape(1, rows, cols, chans)


def solution(mesh):
    in_specs = (
        P("groups", "tile", None, "date", None),
        P("groups", "tile", None, "date"),
        P(("groups", "date")),
        P("head"),
        P(None, "head"),
        P(None, "head"),
        P(None, None, None, "head"),
        P(None, None, None, "head"),
    )
    out_specs = P(("groups", "date"), "tile", None, "head")
    body = functools.partial(local, mesh.shape["date"], mesh.shape["tile"])
    return jax.shard_map(body, mesh=mesh, in_specs=in_specs, out_specs=out_specs, check_vma=False)
```

```python
import functools
import math

import jax
import jax.numpy as jnp
from jax import lax
from jax.experimental import pallas as pl
from jax.experimental.pallas import tpu as pltpu
from jax.sharding import PartitionSpec as P

HSIZE = 32
HALO = 2
MESH = pl.DeviceIdType.MESH
F32, BF16 = jnp.float32, jnp.bfloat16


cloud_penalty = 6.0


def iota(shape, dim):
    return lax.broadcasted_iota(jnp.int32, shape, dim)


def frequencies(width):
    pair = iota((1, width), 1) // 2
    freq = jnp.ones((1, width), F32)
    bit = 1
    while bit < width // 2:
        freq = jnp.where((pair // bit) % 2 == 1, freq * F32(1000.0 ** (-2.0 * bit / width)), freq)
        bit *= 2
    return freq


def encoding(days, width):
    angle = days * frequencies(width)
    turns = jnp.floor(angle * F32(2.0 / math.pi) + F32(0.5))
    rest = angle - turns * F32(1.5703125)
    rest = rest - turns * F32(4.837512969970703125e-4)
    rest = rest - turns * F32(7.54978995489188216e-8)
    square = rest * rest
    sine = (F32(-1.9515295891e-4) * square + F32(8.3321608736e-3)) * square + F32(-1.6666654611e-1)
    sine = sine * square * rest + rest
    cosine = (F32(2.443315711809948e-5) * square + F32(-1.388731625493765e-3)) * square
    cosine = (cosine + F32(4.166664568298827e-2)) * square * square - F32(0.5) * square + F32(1.0)
    quadrant = turns.astype(jnp.int32) + iota(angle.shape, 1) % 2
    value = jnp.where(quadrant % 2 == 1, cosine, sine)
    return jnp.where((quadrant // 2) % 2 == 1, -value, value)


def split(value, parts):
    terms = []
    for _ in range(parts):
        term = value.astype(BF16)
        terms.append(term)
        value = value - term.astype(F32)
    return terms


def shifted(field, cols):
    count = field.shape[0]
    col = iota(field.shape, 0) % cols
    left = jnp.where(col == 0, 0.0, pltpu.roll(field, 1, 0))
    right = jnp.where(col == cols - 1, 0.0, pltpu.roll(field, count - 1, 0))
    return left, field, right


def windows(field, cols):
    sides = shifted(field, cols)
    count = field.shape[0] - 2 * cols
    return jnp.concatenate(
        [side[arow * cols : arow * cols + count].astype(BF16) for arow in range(3) for side in sides],
        axis=1,
    )


def kernel(
    sizes,
    tokens,
    mask,
    days,
    query,
    key_weight,
    value_weight,
    conv_first,
    conv_second,
    out,
    tok_v,
    mask_v,
    days_v,
    query_v,
    wk_v,
    wv_v,
    w1_v,
    w2_v,
    proj_v,
    enc_v,
    part_s,
    part_r,
    low_r,
    high_r,
    pool_v,
    tok_sem,
    in_sem,
    w1_send,
    w1_recv,
    part_send,
    part_recv,
    pool_send,
    pool_recv,
):
    n, slabs, rows, cols, dates, width = sizes
    pixels = rows * cols
    chans = query.shape[1]
    date, slab, head = lax.axis_index("date"), lax.axis_index("tile"), lax.axis_index("head")
    other = 1 - head
    has_up, has_down = slab > 0, slab < slabs - 1

    def tile_at(step):
        return lax.rem(date + 1 + step, n)

    def tok_copy(tile):
        return pltpu.make_async_copy(tokens.at[tile], tok_v.at[tile], tok_sem.at[tile])

    barrier = pltpu.get_barrier_semaphore()

    def signal(where):
        pl.semaphore_signal(barrier, inc=1, device_id=where, device_id_type=MESH)

    @pl.loop(1, n)
    def _(step):
        signal({"date": lax.rem(date + step, n)})

    for has, off in ((has_up, -1), (has_down, 1)):

        @pl.when(has)
        def _(off=off):
            @pl.loop(0, n)
            def _(step):
                signal({"date": lax.rem(date + step, n), "tile": slab + off})

    signal({"head": other})

    loads = [
        pltpu.make_async_copy(days, days_v, in_sem.at[0]),
        pltpu.make_async_copy(query, query_v, in_sem.at[1]),
        pltpu.make_async_copy(key_weight, wk_v, in_sem.at[2]),
        pltpu.make_async_copy(value_weight, wv_v, in_sem.at[3]),
        pltpu.make_async_copy(mask, mask_v, in_sem.at[4]),
        pltpu.make_async_copy(conv_first, w1_v.at[head], in_sem.at[5]),
        pltpu.make_async_copy(conv_second, w2_v, in_sem.at[6]),
    ]
    for load in loads[:5]:
        load.start()

    @pl.loop(0, n)
    def _(step):
        tok_copy(tile_at(step)).start()

    for load in loads[5:]:
        load.start()

    loads[0].wait()
    day_row = days_v[...].astype(F32)
    eye = iota((dates, dates), 0) == iota((dates, dates), 1)
    day_col = jnp.sum(jnp.where(eye, jnp.broadcast_to(day_row, (dates, dates)), 0.0), axis=1, keepdims=True)
    enc_v[...] = encoding(day_col, width)

    same_head = iota((chans, chans), 0) // HSIZE == iota((chans, chans), 1) // HSIZE
    blocks = jnp.where(same_head, 1.0, 0.0).astype(BF16)
    for load in loads[1:4]:
        load.wait()
    scaled = wk_v[...].astype(F32) * (query_v[...] * F32(1.0 / math.sqrt(HSIZE)))
    folded = jnp.zeros((width, chans), F32)
    for term in split(scaled, 3):
        folded = folded + jnp.dot(term, blocks, preferred_element_type=F32)
    high, low = split(folded, 2)
    proj_v[:, :chans] = wv_v[...]
    proj_v[:, chans : 2 * chans] = high
    proj_v[:, 2 * chans :] = low
    loads[4].wait()

    lane = iota((8, chans), 1) % HSIZE // 4
    ones = jnp.ones((dates, chans), BF16)

    halo = HALO * cols
    ends = halo + 16

    def part_copy(way, tile, slot):
        start, count = ((0, pixels + 16), (0, ends), (pixels - halo, ends))[way]
        return pltpu.make_async_remote_copy(
            src_ref=part_s.at[tile, pl.ds(start, count)],
            dst_ref=(part_r, low_r, high_r)[way].at[slot],
            send_sem=part_send.at[way, tile],
            recv_sem=part_recv.at[way, slot],
            device_id=({"date": tile}, {"date": tile, "tile": slab - 1}, {"date": tile, "tile": slab + 1})[way],
            device_id_type=MESH,
        )

    def beside(fn):
        @pl.when(has_up)
        def _():
            fn(1)

        @pl.when(has_down)
        def _():
            fn(2)

    def attend(tile):
        feats = tok_v[tile].astype(F32).reshape(pixels, dates, width)
        inputs = (feats + enc_v[...][None]).astype(BF16).reshape(pixels * dates, width)
        both = jnp.dot(inputs, proj_v[...], preferred_element_type=F32)
        clear = jnp.broadcast_to(mask_v[tile].astype(F32)[:, None, :], (pixels, dates, dates))
        cloud = jnp.where(eye[None], F32(-cloud_penalty) * (1.0 - clear), 0.0).astype(BF16)
        cloud = jnp.dot(cloud.reshape(pixels * dates, dates), ones, preferred_element_type=F32)
        score = both[:, chans : 2 * chans] + both[:, 2 * chans :] + cloud
        score = score.reshape(pixels, dates, chans)
        vals = both[:, :chans].reshape(pixels, dates, chans)
        top = sum(term.astype(F32) for term in split(jnp.max(score, axis=1), 2))
        expo = jnp.exp(score - top[:, None, :])
        total = jnp.sum(expo, axis=1)
        sums = jnp.sum(expo * vals, axis=1)
        groups = pixels // 8
        stats = top[:8]
        for group in range(groups):
            stats = jnp.where(lane == group, top[group * 8 : group * 8 + 8], stats)
            stats = jnp.where(lane == group + groups, total[group * 8 : group * 8 + 8], stats)
        part_s[tile, :halo] = sums[:halo].astype(BF16)
        part_s[tile, halo:ends] = jnp.concatenate(split(stats, 2), axis=0)
        part_s[tile, ends:] = sums[halo:].astype(BF16)

    def send(step):
        part_copy(0, tile_at(step), date).start()
        beside(lambda way: part_copy(way, tile_at(step), date).start())

    tok_copy(tile_at(0)).wait()
    attend(tile_at(0))
    sides = has_up.astype(jnp.int32) + has_down.astype(jnp.int32)
    pl.semaphore_wait(barrier, n + n * sides)
    send(0)

    @pl.loop(1, n - 1)
    def _(step):
        tok_copy(tile_at(step)).wait()
        attend(tile_at(step))
        send(step)

    tok_copy(date).wait()
    attend(date)
    beside(lambda way: part_copy(way, date, date).start())
    w1_copy = pltpu.make_async_remote_copy(
        src_ref=conv_first,
        dst_ref=w1_v.at[head],
        send_sem=w1_send,
        recv_sem=w1_recv,
        device_id={"head": other},
        device_id_type=MESH,
    )
    w1_copy.start()
    part_r[date] = part_s[date]

    groups = pixels // 8

    def merge(parts, at, stat_at, first, count):
        def stat_of(source):
            both = parts[source, stat_at : stat_at + 16].astype(F32)
            return both[:8] + both[8:]

        stats = [stat_of(source) for source in range(n)]
        best = functools.reduce(jnp.maximum, stats)
        scales = [jnp.exp(stat - best) for stat in stats]
        tots = sum(scale * pltpu.roll(stat, chans - HSIZE // 2, 1) for scale, stat in zip(scales, stats))
        inverse = 1.0 / tots
        total = jnp.zeros((8 * count, chans), F32)
        for source in range(n):
            weight = scales[source] * inverse
            wides = []
            for group in range(first, first + count):
                wide = weight if group == 0 else pltpu.roll(weight, chans - 4 * group, 1)
                wide = jnp.where(lane == 0, wide, 0.0)
                for step in (4, 8, 16):
                    wide = wide + pltpu.roll(wide, step, 1)
                wides.append(wide)
            sums = parts[source, at : at + 8 * count].astype(F32)
            total = total + jnp.concatenate(wides, axis=0) * sums
        return total.astype(BF16)

    half = groups // 2

    def pool_copy(index, start, count):
        return pltpu.make_async_remote_copy(
            src_ref=pool_v.at[head, pl.ds(start, count)],
            dst_ref=pool_v.at[head, pl.ds(start, count)],
            send_sem=pool_send.at[index],
            recv_sem=pool_recv.at[index],
            device_id={"head": other},
            device_id_type=MESH,
        )

    high_copy = pool_copy(0, 0, halo)
    own_copy = pool_copy(1, halo, pixels)
    low_copy = pool_copy(2, halo + pixels, halo)

    @pl.loop(1, n)
    def _(step):
        part_copy(0, date, lax.rem(date + step, n)).wait_recv()

    pool_v[head, halo : 2 * halo] = merge(part_r, 0, halo, 0, half)
    pool_v[head, 2 * halo : 3 * halo] = merge(part_r, ends, halo, half, half)
    own_copy.start()

    zeros = jnp.zeros((2, halo, chans), BF16)

    @pl.when(jnp.logical_not(has_up))
    def _():
        pool_v[:, :halo] = zeros

    @pl.when(jnp.logical_not(has_down))
    def _():
        pool_v[:, halo + pixels :] = zeros

    @pl.when(has_up)
    def _():
        @pl.loop(0, n)
        def _(source):
            part_copy(2, date, source).wait_recv()

        pool_v[head, :halo] = merge(high_r, 16, 0, half, half)
        high_copy.start()

    @pl.when(has_down)
    def _():
        @pl.loop(0, n)
        def _(source):
            part_copy(1, date, source).wait_recv()

        pool_v[head, halo + pixels :] = merge(low_r, 0, halo, 0, half)
        low_copy.start()

    for load in loads[5:]:
        load.wait()
    w1_copy.wait()
    own_copy.wait_recv()

    @pl.when(has_up)
    def _():
        high_copy.wait_recv()

    @pl.when(has_down)
    def _():
        low_copy.wait_recv()

    field = jnp.concatenate([pool_v[0], pool_v[1]], axis=1).astype(F32)
    first = jnp.concatenate([w1_v[0], w1_v[1]], axis=1)
    hidden = jnp.dot(windows(field, cols), first, preferred_element_type=F32)
    hidden = jnp.maximum(hidden, 0.0).astype(BF16).astype(F32)
    place = iota(hidden.shape, 0) // cols + (slab * rows - 1)
    hidden = jnp.where((place >= 0) & (place < slabs * rows), hidden, 0.0)
    out[...] = jnp.dot(windows(hidden, cols), w2_v[...], preferred_element_type=F32).astype(BF16)

    @pl.loop(0, n - 1)
    def _(step):
        part_copy(0, tile_at(step), date).wait_send()

    def sent(way):
        @pl.loop(0, n)
        def _(tile):
            part_copy(way, tile, date).wait_send()

    beside(sent)
    own_copy.wait_send()

    @pl.when(has_up)
    def _():
        high_copy.wait_send()

    @pl.when(has_down)
    def _():
        low_copy.wait_send()


def local(n, slabs, tokens, cloud_mask, day_of_year, query, key_weight, value_weight, conv_first, conv_second):
    tiles, rows, cols, dates, width = tokens.shape
    pixels = rows * cols
    chans = query.shape[0]
    depth = 9 * width
    hbm = pl.BlockSpec(memory_space=pltpu.HBM)
    vmem = pl.BlockSpec(memory_space=pltpu.VMEM)
    result = pl.pallas_call(
        functools.partial(kernel, (n, slabs, rows, cols, dates, width)),
        out_shape=jax.ShapeDtypeStruct((pixels, chans), BF16),
        in_specs=[hbm] * 8,
        out_specs=vmem,
        scratch_shapes=[
            pltpu.VMEM((n, pixels * dates, width), BF16),
            pltpu.VMEM((n, pixels, dates), jnp.int32),
            pltpu.VMEM((1, dates), jnp.int32),
            pltpu.VMEM((1, chans), F32),
            pltpu.VMEM((width, chans), BF16),
            pltpu.VMEM((width, chans), BF16),
            pltpu.VMEM((2, depth, chans), BF16),
            pltpu.VMEM((depth, chans), BF16),
            pltpu.VMEM((width, 3 * chans), BF16),
            pltpu.VMEM((dates, width), F32),
            pltpu.VMEM((n, pixels + 16, chans), BF16),
            pltpu.VMEM((n, pixels + 16, chans), BF16),
            pltpu.VMEM((n, HALO * cols + 16, chans), BF16),
            pltpu.VMEM((n, HALO * cols + 16, chans), BF16),
            pltpu.VMEM((2, pixels + 2 * HALO * cols, chans), BF16),
            pltpu.SemaphoreType.DMA((n,)),
            pltpu.SemaphoreType.DMA((7,)),
            pltpu.SemaphoreType.DMA,
            pltpu.SemaphoreType.DMA,
            pltpu.SemaphoreType.DMA((3, n)),
            pltpu.SemaphoreType.DMA((3, n)),
            pltpu.SemaphoreType.DMA((3,)),
            pltpu.SemaphoreType.DMA((3,)),
        ],
        compiler_params=pltpu.CompilerParams(
            collective_id=0, has_side_effects=True, vmem_limit_bytes=60 * 1024 * 1024
        ),
    )(
        tokens.reshape(tiles, pixels * dates, width),
        cloud_mask.reshape(tiles, pixels, dates),
        day_of_year.reshape(1, dates),
        query.reshape(1, chans),
        key_weight,
        value_weight,
        conv_first.reshape(depth, chans),
        conv_second.reshape(depth, chans),
    )
    return result.reshape(1, rows, cols, chans)


def solution(mesh):
    in_specs = (
        P("groups", "tile", None, "date", None),
        P("groups", "tile", None, "date"),
        P(("groups", "date")),
        P("head"),
        P(None, "head"),
        P(None, "head"),
        P(None, None, None, "head"),
        P(None, None, None, "head"),
    )
    out_specs = P(("groups", "date"), "tile", None, "head")
    body = functools.partial(local, mesh.shape["date"], mesh.shape["tile"])
    return jax.shard_map(body, mesh=mesh, in_specs=in_specs, out_specs=out_specs, check_vma=False)
```
